32 devices in a mesh: enc: 4 (over z), grp: 8 (over y, x, core).
Axes of the slice: x: 2, y: 2, z: 4, core: 2. Of those that a mesh axis runs over, the one named last changes fastest.
Arguments:
- query_raw: bfloat16 [6144, 1024], P(('enc', 'grp')), may hold values from -6 to 6
- key_raw: bfloat16 [6144, 1024], P(('enc', 'grp')), may hold values from -6 to 6
- value_rows: bfloat16 [6144, 1024], P(('enc', 'grp')), may hold values from -6 to 6
- out_cotangent: bfloat16 [6144, 1024], P(('enc', 'grp')), may hold values from -6 to 6
- image_ids: int32 [6144], P(('enc', 'grp')), may hold values from 0 to 15, as said below
- owners: int32 [8, 4, 12], P('grp'), may hold values from -1 to 3, as said below
- gains: float32 [2, 1024], replicated, may hold values from 0.1 to 1.9
Outputs:
- query_grad: bfloat16 [4096, 1024], P(('enc', 'grp'))
- key_grad: bfloat16 [4096, 1024], P(('enc', 'grp'))
- value_grad: bfloat16 [4096, 1024], P(('enc', 'grp'))
- gain_grad: float32 [2, 1024], P(None, 'grp')
The draws below stay inside these ranges and needn't reach their ends.
Inputs may be any that keep to these rules, and one draw needn't show every extreme that they name: `image_ids`: inside each piece of 16 rows the number is 0 at the first row and rises by 0 or 1 from row to row. `owners`: A loader's live slots come first; a loader gives at most 3 pieces to one owner and some loader of each group gives exactly 3 to every owner; every owner receives exactly 8 pieces of its group.
All inputs are finite; a program needn't handle non-finite values.
Results may differ from the reference program's by a relative error of at most 0.0073.
Values may be sent and summed in bfloat16 or wider, within the bound.
A program may use at most 64 MiB of HBM per device.

```python
import jax
import jax.numpy as jnp
from jax import lax

HEADS = 16
HD = 64
F = 1024
PIECE = 16
PMAX = 12
P_OWN = 8
ROWS = 6144
OUT_ROWS = 4096
N_ENC = 4
N_GRP = 8


def draw_owners(key, part):
    group_keys = jax.random.split(key, N_GRP)

    def one_group(group_key):
        first_key, second_key, third_key = jax.random.split(group_key, 3)
        pair_count = N_ENC // 2
        largest_shift = PMAX - P_OWN
        shifts = jax.random.randint(first_key, (pair_count,), 0, largest_shift + 1)
        forced = jax.random.randint(second_key, (), 0, pair_count)
        shifts = jnp.where(jnp.arange(pair_count) == forced, largest_shift, shifts)
        direction = jax.random.randint(third_key, (pair_count,), 0, 2) * 2 - 1
        counts = jnp.stack([P_OWN + direction * shifts, P_OWN - direction * shifts], 1).reshape(N_ENC)
        live_flags = (jnp.arange(PMAX)[None, :] < counts[:, None]).astype(jnp.int32)
        flat_live = live_flags.reshape(-1)
        running = jnp.cumsum(flat_live) - flat_live
        owner_ids = jnp.where(flat_live > 0, running % N_ENC, -1)
        return owner_ids.reshape(N_ENC, PMAX).astype(jnp.int32)
    return jax.vmap(one_group)(group_keys)


def draw_image_ids(key, part):
    new_image = (jax.random.randint(key, (ROWS // PIECE, PIECE), 0, 8) == 0).astype(jnp.int32)
    first_piece = jnp.arange(ROWS // PIECE)[:, None] % PMAX == 0
    new_image = jnp.where(first_piece, 1, new_image)
    new_image = new_image.at[:, 0].set(1)
    image_num = jnp.cumsum(new_image, 1) - 1
    return image_num.reshape(ROWS).astype(jnp.int32)


def strengthened(result, key, source, target, parts, factor):
    owner, partner = [(jnp.arange(result.shape[dim]) // (result.shape[dim] // parts)).reshape([-1 if axis == dim else 1 for axis in range(result.ndim)]) for dim in (source, target)]
    chosen = jax.random.permutation(key, parts)[partner]
    strong = (owner == chosen) | (owner == (partner + parts // 2) % parts)
    return jnp.where(strong, factor * result, result)


def level_of(rng, extent, pieces, low, top_value):
    loudness = 1.0
    for dim, blocks in pieces:
        steps = jax.random.uniform(jax.random.fold_in(jax.random.fold_in(rng, 6), dim), (blocks,), jnp.float32, low / len(pieces), top_value / len(pieces))
        loudness = loudness * jnp.repeat(jnp.exp(steps), extent[dim] // blocks).reshape((-1,) + (1,) * (len(extent) - 1 - dim))
    return loudness


def scatter_about(key, extent, scale, bound, cuts=(), kind=jnp.bfloat16):
    gain = level_of(key, extent, cuts, -0.22, 0.18) if cuts else 1.0
    entries = jax.random.normal(key, extent, jnp.float32) * scale * gain
    return jnp.minimum(jnp.maximum(entries, -bound), bound).astype(kind)


def heavy_noise(stream_key, extent, scale, most, cuts, heavy, kind=jnp.bfloat16):
    values = scale * jax.random.normal(stream_key, extent, jnp.float32)
    if cuts:
        values = values * level_of(stream_key, extent, cuts, -0.22, 0.18)
    return jnp.clip(strengthened(values, jax.random.fold_in(stream_key, 3), *heavy), -most, most).astype(kind)


def setup_inputs(seed: int = 0) -> dict:
    seeds = jax.random.split(jax.random.key(seed), 8)
    query_raw = scatter_about(seeds[0], (ROWS, F), 1.0, 6.0, ((0, 32),))
    key_raw = scatter_about(seeds[1], (ROWS, F), 1.0, 6.0, ((0, 32),))
    value_rows = scatter_about(seeds[2], (ROWS, F), 1.0, 6.0, ((0, 32),))
    out_cotangent = heavy_noise(seeds[3], (ROWS, F), 1.0, 6.0, ((0, 32),), (0, 1, 32, 2.75))
    image_ids = draw_image_ids(jax.random.fold_in(seeds[7], 71), 0)
    owners = draw_owners(jax.random.fold_in(seeds[7], 71), 0)
    gains = jnp.clip(1.0 + 0.18 * jax.random.normal(seeds[6], (2, F), jnp.float32), 0.1, 1.9)
    return {"query_raw": query_raw, "key_raw": key_raw, "value_rows": value_rows, "out_cotangent": out_cotangent, "image_ids": image_ids, "owners": owners, "gains": gains}


epsilon = 1e-05

def product(form, left, right):
    return jnp.einsum(form, left.astype(jnp.float32), right.astype(jnp.float32))

def normalize(blocks, gain_row):
    num_pieces = blocks.shape[0]
    values_four = blocks.astype(jnp.float32).reshape(num_pieces, PIECE, HEADS, HD)
    centred = values_four - lax.optimization_barrier(jnp.mean(values_four, -1, keepdims=True))
    inv_scale = lax.rsqrt(lax.optimization_barrier(jnp.mean(centred * centred, -1, keepdims=True)) + epsilon)
    normed = centred * inv_scale
    return (normed, inv_scale, (normed * gain_row).astype(jnp.bfloat16))

def norm_back(d_hat, normed, inv_scale, gain_row, live_flags):
    d_norm = d_hat * gain_row
    d_input = inv_scale * (d_norm - lax.optimization_barrier(jnp.mean(d_norm, -1, keepdims=True)) - normed * lax.optimization_barrier(jnp.mean(d_norm * normed, -1, keepdims=True)))
    gain_term = lax.optimization_barrier(jnp.sum(d_hat * normed * live_flags[:, None, None, None], (0, 1)))
    return (d_input, gain_term.reshape(-1))

def piece_grads(query_rows, key_rows, value_rows, cotangent, image_num, gains, live_flags):
    num_pieces = query_rows.shape[0]
    four_shape = (num_pieces, PIECE, HEADS, HD)
    gain_query = gains[0].reshape(HEADS, HD)
    gain_key = gains[1].reshape(HEADS, HD)
    q_norm, q_scale, q_hat = normalize(query_rows, gain_query)
    k_norm, k_scale, k_hat = normalize(key_rows, gain_key)
    values_four = value_rows.reshape(four_shape)
    cot_four = cotangent.reshape(four_shape)
    factor = HD ** (-0.5)
    scores = product('bihd,bjhd->bhij', q_hat, k_hat) * factor
    same_image = image_num[:, None, :, None] == image_num[:, None, None, :]
    weights = jnp.where(same_image, jnp.exp(scores), 0.0)
    probs = weights / lax.optimization_barrier(jnp.sum(weights, -1, keepdims=True))
    probs_b = probs.astype(jnp.bfloat16)
    attended = product('bhij,bjhd->bihd', probs_b, values_four)
    row_delta = lax.optimization_barrier(jnp.sum(cot_four.astype(jnp.float32) * attended, -1))
    d_value = product('bhij,bihd->bjhd', probs_b, cot_four).astype(jnp.bfloat16)
    d_prob = product('bihd,bjhd->bhij', cot_four, values_four)
    d_score = (probs * (d_prob - jnp.transpose(row_delta, (0, 2, 1))[..., None]) * factor).astype(jnp.bfloat16)
    d_qhat = product('bhij,bjhd->bihd', d_score, k_hat)
    d_khat = product('bhij,bihd->bjhd', d_score, q_hat)
    d_query, term_query = norm_back(d_qhat, q_norm, q_scale, gain_query, live_flags)
    d_key, term_key = norm_back(d_khat, k_norm, k_scale, gain_key, live_flags)
    flat_shape = (num_pieces, PIECE, HEADS * HD)
    return (d_query.reshape(flat_shape).astype(jnp.bfloat16), d_key.reshape(flat_shape).astype(jnp.bfloat16), d_value.reshape(flat_shape), jnp.stack([term_query, term_key]))

def reference(query_raw, key_raw, value_rows, out_cotangent, image_ids, owners, gains):
    dev_blocks = N_ENC * N_GRP
    feat = HEADS * HD
    owner_piece = jnp.transpose(owners, (1, 0, 2)).reshape(dev_blocks, PMAX)
    live_all = (owner_piece >= 0).astype(jnp.float32)

    def device_step(total, inputs):
        q_b, k_b, v_b, d_b, i_b, l_b = inputs
        d_q, d_k, d_v, terms = piece_grads(q_b, k_b, v_b, d_b, i_b, gains, l_b)
        return (total + terms, (d_q, d_k, d_v))
    shaped = (dev_blocks, PMAX, PIECE, feat)
    total, outs = lax.scan(device_step, jnp.zeros((2, feat), jnp.float32), (query_raw.reshape(shaped), key_raw.reshape(shaped), value_rows.reshape(shaped), out_cotangent.reshape(shaped), image_ids.reshape(dev_blocks, PMAX, PIECE), live_all))
    group_view = owners.reshape(N_GRP, N_ENC * PMAX)
    owner_hit = (group_view[..., None] == jnp.arange(N_ENC, dtype=jnp.int32)[None, None, :]).astype(jnp.int32)
    slot_rank = lax.optimization_barrier(jnp.sum((jnp.cumsum(owner_hit, 1) - owner_hit) * owner_hit, -1))
    group_index = jnp.arange(N_GRP, dtype=jnp.int32)[:, None]
    out_pieces = OUT_ROWS // PIECE
    target = jnp.where(group_view >= 0, (group_view * N_GRP + group_index) * P_OWN + slot_rank, out_pieces)
    target = jnp.transpose(target.reshape(N_GRP, N_ENC, PMAX), (1, 0, 2)).reshape(-1).astype(jnp.int32)
    results = []
    for grads in outs:
        placed = jnp.zeros((out_pieces, PIECE, feat), jnp.bfloat16)
        placed = placed.at[target].set(grads.reshape(-1, PIECE, feat), mode='drop')
        results.append(placed.reshape(OUT_ROWS, feat))
    gain_grad = total / jnp.sqrt(jnp.float32(OUT_ROWS))
    return (results[0], results[1], results[2], gain_grad)
```

```python
import functools
import math

import jax
import jax.numpy as jnp
from jax import lax
from jax.experimental import pallas as pl
from jax.experimental.pallas import tpu as pltpu
from jax.sharding import PartitionSpec as P

HD = 64
PIECE = 16
P_OWN = 8
LANES = 128
UNIT = 4
EPS = 1e-05
FACTOR = HD ** (-0.5)
MESH = pl.DeviceIdType.MESH
BF = jnp.bfloat16
F32 = jnp.float32


def dot(a, b, da=1, db=0):
    return lax.dot_general(a, b, (((da,), (db,)), ((), ())), preferred_element_type=F32)


def xor(index, flip):
    out, bit = 0, 1
    while bit <= flip or bit == 1:
        have = lax.rem(index // bit, 2)
        out = out + bit * ((1 - have) if flip & bit else have)
        bit *= 2
    return out + (index // bit) * bit


def partners(me, count):
    if count & (count - 1) == 0:
        flips = list(range(count // 2, count)) + list(range(count // 2 - 1, 0, -1))
        return [(xor(me, f), xor(me, f)) for f in flips] + [(me, me)]
    offs = list(range(count // 2, count)) + list(range(count // 2 - 1, 0, -1))
    return [
        (lax.rem(me + o, count), lax.rem(me + count - o, count)) for o in offs
    ] + [(me, me)]


def kernel(
    n, groups, pmax, q_hbm, k_hbm, v_hbm, d_hbm, ids_ref, plan_ref, gains_ref,
    oq_ref, ok_ref, ov_ref, og_ref,
    q_ref, k_ref, v_ref, d_ref, send, recv, acc, gpart, grecv, erecv,
    in_sem, own_sem, send_sem, recv_sem, gs_sem, gr_sem, es_sem, er_sem,
):
    feat = q_ref.shape[1]
    per = pmax // n
    me = lax.axis_index("enc")
    grp = lax.axis_index("grp")
    width = og_ref.shape[1]

    loads = [
        pltpu.make_async_copy(src, dst, in_sem.at[i])
        for i, (src, dst) in enumerate(
            ((q_hbm, q_ref), (k_hbm, k_ref), (v_hbm, v_ref), (d_hbm, d_ref))
        )
    ]
    for load in loads:
        load.start()
    barrier = pltpu.get_barrier_semaphore()
    for off in range(1, n):
        pl.semaphore_signal(
            barrier, inc=1, device_id={"enc": lax.rem(me + off, n)}, device_id_type=MESH
        )
    for off in range(1, groups):
        pl.semaphore_signal(
            barrier, inc=1, device_id={"grp": lax.rem(grp + off, groups)}, device_id_type=MESH
        )

    steps = partners(me, n)
    plan = [plan_ref[0, me, j] for j in range(pmax)]
    slots = []
    for to, _ in steps:
        count = 0
        source = [0] * per
        for j in range(pmax):
            hit = plan[j] == to
            for r in range(per):
                source[r] = jnp.where(jnp.logical_and(hit, count == r), j, source[r])
            count = count + hit.astype(jnp.int32)
        slots += [(source[r], jnp.where(count > r, 1, 0)) for r in range(per)]

    rows = UNIT * PIECE
    row = lax.broadcasted_iota(jnp.int32, (rows, LANES), 0)
    lane = lax.broadcasted_iota(jnp.int32, (rows, LANES), 1)
    first = lane < HD
    m0 = first.astype(F32).astype(BF)
    m1 = (1.0 - first.astype(F32)).astype(BF)
    brow = lax.broadcasted_iota(jnp.int32, (LANES, LANES), 0)
    bcol = lax.broadcasted_iota(jnp.int32, (LANES, LANES), 1)
    blk = ((brow // HD) == (bcol // HD)).astype(F32).astype(BF)
    blk2 = jnp.concatenate([blk, blk], 0)

    def seg(x):
        high = x.astype(BF)
        low = (x - high.astype(F32)).astype(BF)
        return dot(jnp.concatenate([high, low], 1), blk2)

    def both(x):
        return jnp.concatenate([x * m0, x * m1], 0)

    def halves(x):
        return jnp.where(first, x[:rows], x[rows:])

    acc[...] = jnp.zeros_like(acc)
    gpart[...] = jnp.zeros_like(gpart)
    for load in loads:
        load.wait()

    def pick(values):
        out = values[-1]
        for i in range(UNIT - 2, -1, -1):
            out = jnp.where(row < (i + 1) * PIECE, values[i], out)
        return out

    def unit(chunk):
        source = [s for s, _ in slots[chunk * UNIT : (chunk + 1) * UNIT]]
        live = pick([f for _, f in slots[chunk * UNIT : (chunk + 1) * UNIT]]) > 0
        starts = [s * PIECE for s in source]
        ids = ids_ref[...]
        wide = ids.shape[1]
        wrow = lax.broadcasted_iota(jnp.int32, (rows, wide), 0)
        wlane = lax.broadcasted_iota(jnp.int32, (rows, wide), 1)
        base = starts[-1]
        for i in range(UNIT - 2, -1, -1):
            base = jnp.where(wrow < (i + 1) * PIECE, starts[i], base)
        chosen = wlane == base + lax.rem(wrow, PIECE)
        number = jnp.sum(jnp.where(chosen, ids, 0).astype(F32), axis=1, keepdims=True)
        chosen = chosen.astype(F32).astype(BF)
        place = (lane - (row // PIECE) * PIECE).astype(F32)
        hot = (place == number).astype(F32).astype(BF)
        same = dot(hot, jnp.concatenate([hot, hot], 0), 1, 1) > 0.5

        def some(half, carry):
            lanes = [
                pl.ds(pl.multiple_of((half * PAIRS + i) * LANES, LANES), LANES)
                for i in range(PAIRS)
            ]

            def take(ref):
                return [dot(chosen, ref[:, ln]).astype(BF) for ln in lanes]

            def normed(xs, g):
                mean = [dot(x, blk) * (1 / HD) for x in xs]
                cen = [x.astype(F32) - m for x, m in zip(xs, mean)]
                var = [seg(c * c) * (1 / HD) for c in cen]
                inv = [lax.rsqrt(v + EPS) for v in var]
                nor = [c * i for c, i in zip(cen, inv)]
                hat = [(x * gg).astype(BF) for x, gg in zip(nor, g)]
                return nor, inv, hat

            gq = [gains_ref[0:1, ln] for ln in lanes]
            gk = [gains_ref[1:2, ln] for ln in lanes]
            nq, iq, hq = normed(take(q_ref), gq)
            nk, ik, hk = normed(take(k_ref), gk)
            cot = [jnp.where(live, x.astype(F32), 0.0).astype(BF) for x in take(d_ref)]
            hk2 = [both(x) for x in hk]
            v2 = [both(x) for x in take(v_ref)]
            score = [dot(a, b, 1, 1) * FACTOR for a, b in zip(hq, hk2)]
            dprob = [dot(a, b, 1, 1) for a, b in zip(cot, v2)]
            weight = [jnp.where(same, jnp.exp(s), 0.0) for s in score]
            total = [seg(w) for w in weight]
            prob = [w / t for w, t in zip(weight, total)]
            probb = [p.astype(BF) for p in prob]
            delta = [seg(p.astype(F32) * x) for p, x in zip(probb, dprob)]
            dscore = [
                (p * (x - y) * FACTOR).astype(BF) for p, x, y in zip(prob, dprob, delta)
            ]
            dval = [halves(dot(p, c, 0, 0)) for p, c in zip(probb, cot)]
            dq = [dot(a, b) for a, b in zip(dscore, hk2)]
            dk = [halves(dot(a, b, 0, 0)) for a, b in zip(dscore, hq)]

            def back(dh, nor, inv, g, where):
                dn = [a * gg for a, gg in zip(dh, g)]
                one = [seg(a) * (1 / HD) for a in dn]
                two = [seg(a * b) * (1 / HD) for a, b in zip(dn, nor)]
                for i, ln in enumerate(lanes):
                    acc[where : where + 8, ln] += jnp.sum(
                        (dh[i] * nor[i]).reshape(rows // 8, 8, LANES), 0
                    )
                return [
                    i * (a - b - c * d) for i, a, b, c, d in zip(inv, dn, one, nor, two)
                ]

            rq = back(dq, nq, iq, gq, 0)
            rk = back(dk, nk, ik, gk, 8)
            for a, result in enumerate((rq, rk, dval)):
                for i in range(PAIRS):
                    at_lane = pl.multiple_of(a * feat + (half * PAIRS + i) * LANES, LANES)
                    send[chunk * rows : (chunk + 1) * rows, pl.ds(at_lane, LANES)] = result[
                        i
                    ].astype(BF)
            return carry

        lax.fori_loop(0, feat // LANES // PAIRS, some, 0)

    copies = []
    for chunk in range(pmax // UNIT):
        unit(chunk)
        if chunk == 0:
            pl.semaphore_wait(barrier, n - 1 + groups - 1)
        low, high = chunk * UNIT, (chunk + 1) * UNIT
        for step in range(n - 1):
            a, b = max(low, step * per), min(high, (step + 1) * per)
            if a >= b:
                continue
            to, frm = steps[step]
            count = (b - a) * PIECE
            shift = (a - step * per) * PIECE
            sem = len(copies)

            def copy(owner_row):
                return pltpu.make_async_remote_copy(
                    src_ref=send.at[pl.ds(a * PIECE, count)],
                    dst_ref=recv.at[
                        pl.ds(pl.multiple_of(owner_row * (per * PIECE) + shift, PIECE), count)
                    ],
                    send_sem=send_sem.at[sem],
                    recv_sem=recv_sem.at[sem],
                    device_id={"enc": to},
                    device_id_type=MESH,
                )

            copy(me).start()
            copies.append((copy(me), copy(frm)))
    own = pltpu.make_async_copy(
        send.at[pl.ds((n - 1) * per * PIECE, per * PIECE)],
        recv.at[pl.ds(pl.multiple_of(me * (per * PIECE), PIECE), per * PIECE)],
        own_sem,
    )
    own.start()

    gq = jnp.sum(acc[0:8, :], 0, keepdims=True)
    gk = jnp.sum(acc[8:16, :], 0, keepdims=True)
    for j in range(groups):
        gpart[j, 0:1, 0:width] = gq[:, j * width : (j + 1) * width]
        gpart[j, 1:2, 0:width] = gk[:, j * width : (j + 1) * width]
    shares = []
    for off in range(1, groups):
        to = lax.rem(grp + off, groups)
        share = pltpu.make_async_remote_copy(
            src_ref=gpart.at[to],
            dst_ref=grecv.at[off],
            send_sem=gs_sem.at[off],
            recv_sem=gr_sem.at[off],
            device_id={"grp": to},
            device_id_type=MESH,
        )
        share.start()
        shares.append(share)
    part = gpart[grp]
    for off, share in enumerate(shares, 1):
        share.wait_recv()
        part = part + grecv[off]
    erecv[me] = part
    sums = []
    for i, (to, frm) in enumerate(steps[:-1]):
        both_ways = [
            pltpu.make_async_remote_copy(
                src_ref=erecv.at[me],
                dst_ref=erecv.at[at],
                send_sem=es_sem.at[i],
                recv_sem=er_sem.at[i],
                device_id={"enc": to},
                device_id_type=MESH,
            )
            for at in (me, frm)
        ]
        both_ways[0].start()
        sums.append(both_ways)
    index = [0] * P_OWN
    start = 0
    for s in range(n):
        got = 0
        for j in range(pmax):
            got = got + (plan_ref[0, s, j] == me).astype(jnp.int32)
        for p in range(P_OWN):
            inside = jnp.logical_and(p >= start, p < start + got)
            index[p] = jnp.where(inside, s * per + p - start, index[p])
        start = start + got
    for out, arrived in sums:
        arrived.wait_recv()
    total = erecv[0]
    for s in range(1, n):
        total = total + erecv[s]
    og_ref[...] = total[0:2, 0:width] / math.sqrt(n * groups * P_OWN * PIECE)

    own.wait()
    for out, arrived in copies:
        arrived.wait_recv()
    orow = lax.broadcasted_iota(jnp.int32, (P_OWN * PIECE, pmax * PIECE), 0)
    olane = lax.broadcasted_iota(jnp.int32, (P_OWN * PIECE, pmax * PIECE), 1)
    base = index[-1] * PIECE
    for p in range(P_OWN - 2, -1, -1):
        base = jnp.where(orow < (p + 1) * PIECE, index[p] * PIECE, base)
    order = (olane == base + lax.rem(orow, PIECE)).astype(F32).astype(BF)
    for a, out in enumerate((oq_ref, ok_ref, ov_ref)):
        for low in range(0, feat, feat // 2):
            high = low + feat // 2
            out[:, low:high] = dot(order, recv[:, a * feat + low : a * feat + high]).astype(BF)
    for out, _ in copies:
        out.wait_send()
    for share in shares:
        share.wait_send()
    for out, _ in sums:
        out.wait_send()


PAIRS = 4


def local(query_raw, key_raw, value_rows, out_cotangent, image_ids, owners, gains):
    n = lax.axis_size("enc")
    groups = lax.axis_size("grp")
    pmax = owners.shape[-1]
    rows, feat = query_raw.shape
    own_rows = P_OWN * PIECE
    vmem = pl.BlockSpec(memory_space=pltpu.VMEM)
    hbm = pl.BlockSpec(memory_space=pl.ANY)
    grad = jax.ShapeDtypeStruct((own_rows, feat), BF)
    dma = pltpu.SemaphoreType.DMA
    many = n + pmax // UNIT
    return pl.pallas_call(
        functools.partial(kernel, n, groups, pmax),
        out_shape=(grad, grad, grad, jax.ShapeDtypeStruct((2, feat // groups), F32)),
        in_specs=[hbm] * 4
        + [vmem, pl.BlockSpec(memory_space=pltpu.SMEM), vmem],
        out_specs=(vmem,) * 4,
        scratch_shapes=[pltpu.VMEM((rows, feat), BF)] * 4
        + [
            pltpu.VMEM((rows, 3 * feat), BF),
            pltpu.VMEM((rows, 3 * feat), BF),
            pltpu.VMEM((16, feat), F32),
            pltpu.VMEM((groups, 8, LANES), F32),
            pltpu.VMEM((groups, 8, LANES), F32),
            pltpu.VMEM((n, 8, LANES), F32),
            dma((4,)),
            dma,
            dma((many,)),
            dma((many,)),
            dma((groups,)),
            dma((groups,)),
            dma((n,)),
            dma((n,)),
        ],
        compiler_params=pltpu.CompilerParams(
            collective_id=0, has_side_effects=True, vmem_limit_bytes=32 * 1024 * 1024
        ),
        cost_estimate=pl.CostEstimate(
            flops=2 * 24 * rows * feat * LANES, bytes_accessed=14 * rows * feat, transcendentals=rows * feat
        ),
    )(query_raw, key_raw, value_rows, out_cotangent, image_ids.reshape(1, rows), owners, gains)


def solution(mesh):
    rows = P(("enc", "grp"), None)
    return jax.shard_map(
        local,
        mesh=mesh,
        in_specs=(rows, rows, rows, rows, P(("enc", "grp")), P("grp", None, None), P()),
        out_specs=(rows, rows, rows, P(None, "grp")),
        check_vma=False,
    )
```

```python
import functools
import math

import jax
import jax.numpy as jnp
from jax import lax
from jax.experimental import pallas as pl
from jax.experimental.pallas import tpu as pltpu
from jax.sharding import PartitionSpec as P

HD = 64
PIECE = 16
P_OWN = 8
LANES = 128
UNIT = 4
EPS = 1e-05
FACTOR = HD ** (-0.5)
MESH = pl.DeviceIdType.MESH
BF = jnp.bfloat16
F32 = jnp.float32


def dot(a, b, da=1, db=0):
    return lax.dot_general(a, b, (((da,), (db,)), ((), ())), preferred_element_type=F32)


def xor(index, flip):
    out, bit = 0, 1
    while bit <= flip or bit == 1:
        have = lax.rem(index // bit, 2)
        out = out + bit * ((1 - have) if flip & bit else have)
        bit *= 2
    return out + (index // bit) * bit


def partners(me, count):
    if count & (count - 1) == 0:
        flips = list(range(count // 2, count)) + list(range(count // 2 - 1, 0, -1))
        return [(xor(me, f), xor(me, f)) for f in flips] + [(me, me)]
    offs = list(range(count // 2, count)) + list(range(count // 2 - 1, 0, -1))
    return [
        (lax.rem(me + o, count), lax.rem(me + count - o, count)) for o in offs
    ] + [(me, me)]


def kernel(
    n, groups, pmax, q_hbm, k_hbm, v_hbm, d_hbm, ids_hbm, plan_hbm, gains_hbm,
    recv, order_hbm, og_hbm,
    q_ref, k_ref, v_ref, d_ref, ids_ref, plan_ref, gains_ref,
    order_ref, og_ref, send, acc, gpart, grecv, erecv,
    in_sem, out_sem, own_sem, send_sem, recv_sem, gs_sem, gr_sem, es_sem, er_sem,
):
    feat = q_ref.shape[1]
    per = pmax // n
    me = lax.axis_index("enc")
    grp = lax.axis_index("grp")
    width = og_ref.shape[1]

    loads = [
        pltpu.make_async_copy(src, dst, in_sem.at[i])
        for i, (src, dst) in enumerate(
            (
                (plan_hbm, plan_ref), (ids_hbm, ids_ref), (gains_hbm, gains_ref),
                (q_hbm, q_ref), (k_hbm, k_ref), (v_hbm, v_ref), (d_hbm, d_ref),
            )
        )
    ]
    for load in loads:
        load.start()
    barrier = pltpu.get_barrier_semaphore()
    for off in range(1, n):
        pl.semaphore_signal(
            barrier, inc=1, device_id={"enc": lax.rem(me + off, n)}, device_id_type=MESH
        )
    for off in range(1, groups):
        pl.semaphore_signal(
            barrier, inc=1, device_id={"grp": lax.rem(grp + off, groups)}, device_id_type=MESH
        )

    steps = partners(me, n)
    loads[0].wait()
    plan = [plan_ref[0, me, j] for j in range(pmax)]
    slots = []
    for to, _ in steps:
        count = 0
        source = [0] * per
        for j in range(pmax):
            hit = plan[j] == to
            for r in range(per):
                source[r] = jnp.where(jnp.logical_and(hit, count == r), j, source[r])
            count = count + hit.astype(jnp.int32)
        slots += [(source[r], jnp.where(count > r, 1, 0)) for r in range(per)]

    rows = UNIT * PIECE
    row = lax.broadcasted_iota(jnp.int32, (rows, LANES), 0)
    lane = lax.broadcasted_iota(jnp.int32, (rows, LANES), 1)
    first = lane < HD
    m0 = first.astype(F32).astype(BF)
    m1 = (1.0 - first.astype(F32)).astype(BF)
    brow = lax.broadcasted_iota(jnp.int32, (LANES, LANES), 0)
    bcol = lax.broadcasted_iota(jnp.int32, (LANES, LANES), 1)
    blk = ((brow // HD) == (bcol // HD)).astype(F32).astype(BF)
    blk2 = jnp.concatenate([blk, blk], 0)

    def seg(x):
        high = x.astype(BF)
        low = (x - high.astype(F32)).astype(BF)
        return dot(jnp.concatenate([high, low], 1), blk2)

    def both(x):
        return jnp.concatenate([x * m0, x * m1], 0)

    def halves(x):
        return jnp.where(first, x[:rows], x[rows:])

    acc[...] = jnp.zeros_like(acc)
    gpart[...] = jnp.zeros_like(gpart)
    for load in loads[1:]:
        load.wait()

    def pick(values):
        out = values[-1]
        for i in range(UNIT - 2, -1, -1):
            out = jnp.where(row < (i + 1) * PIECE, values[i], out)
        return out

    def unit(chunk, leave):
        source = [s for s, _ in slots[chunk * UNIT : (chunk + 1) * UNIT]]
        live = pick([f for _, f in slots[chunk * UNIT : (chunk + 1) * UNIT]]) > 0
        starts = [s * PIECE for s in source]
        ids = ids_ref[...]
        wide = ids.shape[1]
        wrow = lax.broadcasted_iota(jnp.int32, (rows, wide), 0)
        wlane = lax.broadcasted_iota(jnp.int32, (rows, wide), 1)
        base = starts[-1]
        for i in range(UNIT - 2, -1, -1):
            base = jnp.where(wrow < (i + 1) * PIECE, starts[i], base)
        chosen = wlane == base + lax.rem(wrow, PIECE)
        number = jnp.sum(jnp.where(chosen, ids, 0).astype(F32), axis=1, keepdims=True)
        chosen = chosen.astype(F32).astype(BF)
        place = (lane - (row // PIECE) * PIECE).astype(F32)
        hot = (place == number).astype(F32).astype(BF)
        same = dot(hot, jnp.concatenate([hot, hot], 0), 1, 1) > 0.5

        def some(half, carry):
            lanes = [
                pl.ds(pl.multiple_of((half * PAIRS + i) * LANES, LANES), LANES)
                for i in range(PAIRS)
            ]

            def take(ref):
                return [dot(chosen, ref[:, ln]).astype(BF) for ln in lanes]

            def normed(xs, g):
                mean = [dot(x, blk) * (1 / HD) for x in xs]
                cen = [x.astype(F32) - m for x, m in zip(xs, mean)]
                var = [seg(c * c) * (1 / HD) for c in cen]
                inv = [lax.rsqrt(v + EPS) for v in var]
                nor = [c * i for c, i in zip(cen, inv)]
                hat = [(x * gg).astype(BF) for x, gg in zip(nor, g)]
                return nor, inv, hat

            gq = [gains_ref[0:1, ln] for ln in lanes]
            gk = [gains_ref[1:2, ln] for ln in lanes]
            nq, iq, hq = normed(take(q_ref), gq)
            nk, ik, hk = normed(take(k_ref), gk)
            cot = [jnp.where(live, x.astype(F32), 0.0).astype(BF) for x in take(d_ref)]
            hk2 = [both(x) for x in hk]
            v2 = [both(x) for x in take(v_ref)]
            score = [dot(a, b, 1, 1) * FACTOR for a, b in zip(hq, hk2)]
            dprob = [dot(a, b, 1, 1) for a, b in zip(cot, v2)]
            weight = [jnp.where(same, jnp.exp(s), 0.0) for s in score]
            total = [seg(w) for w in weight]
            prob = [w / t for w, t in zip(weight, total)]
            probb = [p.astype(BF) for p in prob]
            delta = [seg(p.astype(F32) * x) for p, x in zip(probb, dprob)]
            dscore = [
                (p * (x - y) * FACTOR).astype(BF) for p, x, y in zip(prob, dprob, delta)
            ]
            dval = [halves(dot(p, c, 0, 0)) for p, c in zip(probb, cot)]
            dq = [dot(a, b) for a, b in zip(dscore, hk2)]
            dk = [halves(dot(a, b, 0, 0)) for a, b in zip(dscore, hq)]

            def back(dh, nor, inv, g, where):
                dn = [a * gg for a, gg in zip(dh, g)]
                one = [seg(a) * (1 / HD) for a in dn]
                two = [seg(a * b) * (1 / HD) for a, b in zip(dn, nor)]
                for i, ln in enumerate(lanes):
                    acc[where : where + 8, ln] += jnp.sum(
                        (dh[i] * nor[i]).reshape(rows // 8, 8, LANES), 0
                    )
                return [
                    i * (a - b - c * d) for i, a, b, c, d in zip(inv, dn, one, nor, two)
                ]

            rq = back(dq, nq, iq, gq, 0)
            rk = back(dk, nk, ik, gk, 8)
            for a, result in enumerate((rq, rk, dval)):
                for i in range(PAIRS):
                    at_lane = pl.multiple_of(half * (3 * part) + a * part + i * LANES, LANES)
                    send[chunk * rows : (chunk + 1) * rows, pl.ds(at_lane, LANES)] = result[
                        i
                    ].astype(BF)
            for copy in leave(half):
                copy.start()
            return carry

        lax.fori_loop(0, halves_count, some, 0)

    part = PAIRS * LANES
    halves_count = feat // part
    spans = []
    for chunk in range(pmax // UNIT):
        low, high = chunk * UNIT, (chunk + 1) * UNIT
        for step in range(n - 1):
            a, b = max(low, step * per), min(high, (step + 1) * per)
            if a < b:
                spans.append((chunk, step, a, b))

    def span_copy(which, half, arriving):
        _, step, a, b = spans[which]
        to, frm = steps[step]
        count = (b - a) * PIECE
        shift = (a - step * per) * PIECE
        at_row = (frm if arriving else me) * (per * PIECE) + shift
        lanes = pl.ds(pl.multiple_of(half * (3 * part), 3 * part), 3 * part)
        return pltpu.make_async_remote_copy(
            src_ref=send.at[pl.ds(a * PIECE, count), lanes],
            dst_ref=recv.at[pl.ds(pl.multiple_of(at_row, PIECE), count), lanes],
            send_sem=send_sem.at[which, half],
            recv_sem=recv_sem.at[which, half],
            device_id={"enc": to},
            device_id_type=MESH,
        )

    pl.semaphore_wait(barrier, n - 1 + groups - 1)
    for chunk in range(pmax // UNIT):
        unit(
            chunk,
            lambda half: [
                span_copy(w, half, False) for w in range(len(spans)) if spans[w][0] == chunk
            ],
        )
    own = pltpu.make_async_copy(
        send.at[pl.ds((n - 1) * per * PIECE, per * PIECE)],
        recv.at[pl.ds(pl.multiple_of(me * (per * PIECE), PIECE), per * PIECE)],
        own_sem,
    )
    own.start()

    gq = jnp.sum(acc[0:8, :], 0, keepdims=True)
    gk = jnp.sum(acc[8:16, :], 0, keepdims=True)
    for j in range(groups):
        gpart[j, 0:1, 0:width] = gq[:, j * width : (j + 1) * width]
        gpart[j, 1:2, 0:width] = gk[:, j * width : (j + 1) * width]
    shares = []
    for off in range(1, groups):
        to = lax.rem(grp + off, groups)
        share = pltpu.make_async_remote_copy(
            src_ref=gpart.at[to],
            dst_ref=grecv.at[off],
            send_sem=gs_sem.at[off],
            recv_sem=gr_sem.at[off],
            device_id={"grp": to},
            device_id_type=MESH,
        )
        share.start()
        shares.append(share)
    mine = gpart[grp]
    for off, share in enumerate(shares, 1):
        share.wait_recv()
        mine = mine + grecv[off]
    erecv[me] = mine
    sums = []
    for i, (to, frm) in enumerate(steps[:-1]):
        both_ways = [
            pltpu.make_async_remote_copy(
                src_ref=erecv.at[me],
                dst_ref=erecv.at[at],
                send_sem=es_sem.at[i],
                recv_sem=er_sem.at[i],
                device_id={"enc": to},
                device_id_type=MESH,
            )
            for at in (me, frm)
        ]
        both_ways[0].start()
        sums.append(both_ways)
    index = [0] * P_OWN
    start = 0
    for s in range(n):
        got = 0
        for j in range(pmax):
            got = got + (plan_ref[0, s, j] == me).astype(jnp.int32)
        for p in range(P_OWN):
            inside = jnp.logical_and(p >= start, p < start + got)
            index[p] = jnp.where(inside, s * per + p - start, index[p])
        start = start + got
    for out, arrived in sums:
        arrived.wait_recv()
    total = erecv[0]
    for s in range(1, n):
        total = total + erecv[s]
    og_ref[...] = total[0:2, 0:width] / math.sqrt(n * groups * P_OWN * PIECE)

    orow = lax.broadcasted_iota(jnp.int32, (P_OWN * PIECE, pmax * PIECE), 0)
    olane = lax.broadcasted_iota(jnp.int32, (P_OWN * PIECE, pmax * PIECE), 1)
    base = index[-1] * PIECE
    for p in range(P_OWN - 2, -1, -1):
        base = jnp.where(orow < (p + 1) * PIECE, index[p] * PIECE, base)
    order_ref[...] = (olane == base + lax.rem(orow, PIECE)).astype(F32).astype(BF)
    small = [
        pltpu.make_async_copy(order_ref, order_hbm, out_sem.at[0]),
        pltpu.make_async_copy(og_ref, og_hbm, out_sem.at[1]),
    ]
    for copy in small:
        copy.start()
    own.wait()
    for copy in small:
        copy.wait()
    for half in range(halves_count):
        for w in range(len(spans)):
            span_copy(w, half, True).wait_recv()
    for half in range(halves_count):
        for w in range(len(spans)):
            span_copy(w, half, False).wait_send()
    for share in shares:
        share.wait_send()
    for out, _ in sums:
        out.wait_send()


def place(recv_hbm, order_hbm, gain, oq, ok, ov, og, recv, order, buf, in_sem, sem):
    feat = oq.shape[1]
    part = PAIRS * LANES
    count = feat // part
    first = pltpu.make_async_copy(order_hbm, order, in_sem.at[3 * count])
    first.start()
    loads = []
    for a in range(3):
        for half in range(count):
            low = half * (3 * part) + a * part
            lanes = slice(low, low + part)
            loads.append(
                pltpu.make_async_copy(
                    recv_hbm.at[:, lanes], recv.at[:, lanes], in_sem.at[a * count + half]
                )
            )
            loads[-1].start()
    copies = [pltpu.make_async_copy(gain, og, sem.at[3])]
    copies[0].start()
    first.wait()
    pick = order[...]
    for a, out in enumerate((oq, ok, ov)):
        for half in range(count):
            loads[a * count + half].wait()
            low = half * (3 * part) + a * part
            buf[a, :, half * part : (half + 1) * part] = dot(
                pick, recv[:, low : low + part]
            ).astype(BF)
        copies.append(pltpu.make_async_copy(buf.at[a], out, sem.at[a]))
        copies[-1].start()
    for copy in copies:
        copy.wait()


PAIRS = 4


def local(query_raw, key_raw, value_rows, out_cotangent, image_ids, owners, gains):
    n = lax.axis_size("enc")
    groups = lax.axis_size("grp")
    pmax = owners.shape[-1]
    rows, feat = query_raw.shape
    own_rows = P_OWN * PIECE
    hbm = pl.BlockSpec(memory_space=pltpu.HBM)
    grad = jax.ShapeDtypeStruct((own_rows, feat), BF)
    gain = jax.ShapeDtypeStruct((2, feat // groups), F32)
    dma = pltpu.SemaphoreType.DMA
    many = n + pmax // UNIT
    halves_count = feat // (PAIRS * LANES)
    arrived, order, share = pl.pallas_call(
        functools.partial(kernel, n, groups, pmax),
        out_shape=(
            jax.ShapeDtypeStruct((rows, 3 * feat), BF),
            jax.ShapeDtypeStruct((own_rows, rows), BF),
            gain,
        ),
        in_specs=[hbm] * 7,
        out_specs=(hbm,) * 3,
        scratch_shapes=[pltpu.VMEM((rows, feat), BF)] * 4
        + [
            pltpu.VMEM((1, rows), jnp.int32),
            pltpu.SMEM(owners.shape, jnp.int32),
            pltpu.VMEM(gains.shape, F32),
            pltpu.VMEM((own_rows, rows), BF),
            pltpu.VMEM(gain.shape, F32),
            pltpu.VMEM((rows, 3 * feat), BF),
            pltpu.VMEM((16, feat), F32),
            pltpu.VMEM((groups, 8, LANES), F32),
            pltpu.VMEM((groups, 8, LANES), F32),
            pltpu.VMEM((n, 8, LANES), F32),
            dma((7,)),
            dma((2,)),
            dma,
            dma((many, halves_count)),
            dma((many, halves_count)),
            dma((groups,)),
            dma((groups,)),
            dma((n,)),
            dma((n,)),
        ],
        compiler_params=pltpu.CompilerParams(
            collective_id=0, has_side_effects=True, vmem_limit_bytes=62 * 1024 * 1024
        ),
        cost_estimate=pl.CostEstimate(
            flops=2 * 24 * rows * feat * LANES,
            bytes_accessed=14 * rows * feat,
            transcendentals=rows * feat,
        ),
    )(query_raw, key_raw, value_rows, out_cotangent, image_ids.reshape(1, rows), owners, gains)
    return pl.pallas_call(
        place,
        out_shape=(grad, grad, grad, gain),
        in_specs=[hbm] * 3,
        out_specs=(hbm,) * 4,
        scratch_shapes=[
            pltpu.VMEM((rows, 3 * feat), BF),
            pltpu.VMEM((own_rows, rows), BF),
            pltpu.VMEM((3, own_rows, feat), BF),
            dma((3 * halves_count + 1,)),
            dma((4,)),
        ],
        compiler_params=pltpu.CompilerParams(vmem_limit_bytes=62 * 1024 * 1024),
    )(arrived, order, share)


def solution(mesh):
    rows = P(("enc", "grp"), None)
    return jax.shard_map(
        local,
        mesh=mesh,
        in_specs=(rows, rows, rows, rows, P(("enc", "grp")), P("grp", None, None), P()),
        out_specs=(rows, rows, rows, P(None, "grp")),
        check_vma=False,
    )
```

```python
import functools
import math

import jax
import jax.numpy as jnp
from jax import lax
from jax.experimental import pallas as pl
from jax.experimental.pallas import tpu as pltpu
from jax.sharding import PartitionSpec as P

HD = 64
PIECE = 16
P_OWN = 8
LANES = 128
UNIT = 4
EPS = 1e-05
FACTOR = HD ** (-0.5)
MESH = pl.DeviceIdType.MESH
BF = jnp.bfloat16
F32 = jnp.float32


def dot(a, b, da=1, db=0):
    return lax.dot_general(a, b, (((da,), (db,)), ((), ())), preferred_element_type=F32)


def xor(index, flip):
    out, bit = 0, 1
    while bit <= flip or bit == 1:
        have = lax.rem(index // bit, 2)
        out = out + bit * ((1 - have) if flip & bit else have)
        bit *= 2
    return out + (index // bit) * bit


def partners(me, count):
    if count & (count - 1) == 0:
        flips = list(range(count // 2, count)) + list(range(count // 2 - 1, 0, -1))
        return [(xor(me, f), xor(me, f)) for f in flips] + [(me, me)]
    offs = list(range(count // 2, count)) + list(range(count // 2 - 1, 0, -1))
    return [
        (lax.rem(me + o, count), lax.rem(me + count - o, count)) for o in offs
    ] + [(me, me)]


def kernel(
    n, groups, pmax, q_hbm, k_hbm, v_hbm, d_hbm, ids_hbm, plan_hbm, gains_hbm,
    recv, order_hbm, og_hbm,
    q_ref, k_ref, v_ref, d_ref, ids_ref, plan_ref, gains_ref,
    order_ref, og_ref, send, acc, gpart, grecv, erecv,
    in_sem, out_sem, own_sem, send_sem, recv_sem, gs_sem, gr_sem, es_sem, er_sem,
):
    feat = q_ref.shape[1]
    per = pmax // n
    me = lax.axis_index("enc")
    grp = lax.axis_index("grp")
    width = og_ref.shape[1]

    loads = [
        pltpu.make_async_copy(src, dst, in_sem.at[i])
        for i, (src, dst) in enumerate(
            (
                (plan_hbm, plan_ref), (ids_hbm, ids_ref), (gains_hbm, gains_ref),
                (q_hbm, q_ref), (k_hbm, k_ref), (v_hbm, v_ref), (d_hbm, d_ref),
            )
        )
    ]
    for load in loads:
        load.start()
    barrier = pltpu.get_barrier_semaphore()
    for off in range(1, n):
        pl.semaphore_signal(
            barrier, inc=1, device_id={"enc": lax.rem(me + off, n)}, device_id_type=MESH
        )
    for off in range(1, groups):
        pl.semaphore_signal(
            barrier, inc=1, device_id={"grp": lax.rem(grp + off, groups)}, device_id_type=MESH
        )

    steps = partners(me, n)
    loads[0].wait()
    plan = [plan_ref[0, me, j] for j in range(pmax)]
    slots = []
    for to, _ in steps:
        count = 0
        source = [0] * per
        for j in range(pmax):
            hit = plan[j] == to
            for r in range(per):
                source[r] = jnp.where(jnp.logical_and(hit, count == r), j, source[r])
            count = count + hit.astype(jnp.int32)
        slots += [(source[r], jnp.where(count > r, 1, 0)) for r in range(per)]

    rows = UNIT * PIECE
    row = lax.broadcasted_iota(jnp.int32, (rows, LANES), 0)
    lane = lax.broadcasted_iota(jnp.int32, (rows, LANES), 1)
    first = lane < HD
    m0 = first.astype(F32).astype(BF)
    m1 = (1.0 - first.astype(F32)).astype(BF)
    brow = lax.broadcasted_iota(jnp.int32, (LANES, LANES), 0)
    bcol = lax.broadcasted_iota(jnp.int32, (LANES, LANES), 1)
    blk = ((brow // HD) == (bcol // HD)).astype(F32).astype(BF)
    blk2 = jnp.concatenate([blk, blk], 0)

    def seg(x):
        high = x.astype(BF)
        low = (x - high.astype(F32)).astype(BF)
        return dot(jnp.concatenate([high, low], 1), blk2)

    def both(x):
        return jnp.concatenate([x * m0, x * m1], 0)

    def halves(x):
        return jnp.where(first, x[:rows], x[rows:])

    acc[...] = jnp.zeros_like(acc)
    gpart[...] = jnp.zeros_like(gpart)
    for load in loads[1:]:
        load.wait()

    def pick(values):
        out = values[-1]
        for i in range(UNIT - 2, -1, -1):
            out = jnp.where(row < (i + 1) * PIECE, values[i], out)
        return out

    def unit(chunk, leave):
        source = [s for s, _ in slots[chunk * UNIT : (chunk + 1) * UNIT]]
        live = pick([f for _, f in slots[chunk * UNIT : (chunk + 1) * UNIT]]) > 0
        starts = [s * PIECE for s in source]
        ids = ids_ref[...]
        wide = ids.shape[1]
        wrow = lax.broadcasted_iota(jnp.int32, (rows, wide), 0)
        wlane = lax.broadcasted_iota(jnp.int32, (rows, wide), 1)
        base = starts[-1]
        for i in range(UNIT - 2, -1, -1):
            base = jnp.where(wrow < (i + 1) * PIECE, starts[i], base)
        chosen = wlane == base + lax.rem(wrow, PIECE)
        number = jnp.sum(jnp.where(chosen, ids, 0).astype(F32), axis=1, keepdims=True)
        chosen = chosen.astype(F32).astype(BF)
        place = (lane - (row // PIECE) * PIECE).astype(F32)
        hot = (place == number).astype(F32).astype(BF)
        same = dot(hot, jnp.concatenate([hot, hot], 0), 1, 1) > 0.5

        def some(half, carry):
            lanes = [
                pl.ds(pl.multiple_of((half * PAIRS + i) * LANES, LANES), LANES)
                for i in range(PAIRS)
            ]

            def take(ref):
                return [dot(chosen, ref[:, ln]).astype(BF) for ln in lanes]

            def normed(xs, g):
                mean = [dot(x, blk) * (1 / HD) for x in xs]
                cen = [x.astype(F32) - m for x, m in zip(xs, mean)]
                var = [seg(c * c) * (1 / HD) for c in cen]
                inv = [lax.rsqrt(v + EPS) for v in var]
                nor = [c * i for c, i in zip(cen, inv)]
                hat = [(x * gg).astype(BF) for x, gg in zip(nor, g)]
                return nor, inv, hat

            gq = [gains_ref[0:1, ln] for ln in lanes]
            gk = [gains_ref[1:2, ln] for ln in lanes]
            nq, iq, hq = normed(take(q_ref), gq)
            nk, ik, hk = normed(take(k_ref), gk)
            cot = [jnp.where(live, x.astype(F32), 0.0).astype(BF) for x in take(d_ref)]
            hk2 = [both(x) for x in hk]
            v2 = [both(x) for x in take(v_ref)]
            score = [dot(a, b, 1, 1) * FACTOR for a, b in zip(hq, hk2)]
            dprob = [dot(a, b, 1, 1) for a, b in zip(cot, v2)]
            weight = [jnp.where(same, jnp.exp(s), 0.0) for s in score]
            total = [seg(w) for w in weight]
            prob = [w / t for w, t in zip(weight, total)]
            probb = [p.astype(BF) for p in prob]
            delta = [seg(p.astype(F32) * x) for p, x in zip(probb, dprob)]
            dscore = [
                (p * (x - y) * FACTOR).astype(BF) for p, x, y in zip(prob, dprob, delta)
            ]
            dval = [halves(dot(p, c, 0, 0)) for p, c in zip(probb, cot)]
            dq = [dot(a, b) for a, b in zip(dscore, hk2)]
            dk = [halves(dot(a, b, 0, 0)) for a, b in zip(dscore, hq)]

            def back(dh, nor, inv, g, where):
                dn = [a * gg for a, gg in zip(dh, g)]
                one = [seg(a) * (1 / HD) for a in dn]
                two = [seg(a * b) * (1 / HD) for a, b in zip(dn, nor)]
                for i, ln in enumerate(lanes):
                    acc[where : where + 8, ln] += jnp.sum(
                        (dh[i] * nor[i]).reshape(rows // 8, 8, LANES), 0
                    )
                return [
                    i * (a - b - c * d) for i, a, b, c, d in zip(inv, dn, one, nor, two)
                ]

            rq = back(dq, nq, iq, gq, 0)
            rk = back(dk, nk, ik, gk, 8)
            for a, result in enumerate((rq, rk, dval)):
                for i in range(PAIRS):
                    at_lane = pl.multiple_of(half * (3 * part) + a * part + i * LANES, LANES)
                    send[chunk * rows : (chunk + 1) * rows, pl.ds(at_lane, LANES)] = result[
                        i
                    ].astype(BF)
            for copy in leave(half):
                copy.start()
            return carry

        lax.fori_loop(0, halves_count, some, 0)

    part = PAIRS * LANES
    halves_count = feat // part
    spans = []
    for chunk in range(pmax // UNIT):
        low, high = chunk * UNIT, (chunk + 1) * UNIT
        for step in range(n - 1):
            a, b = max(low, step * per), min(high, (step + 1) * per)
            if a < b:
                spans.append((chunk, step, a, b))

    def span_copy(which, half, arriving):
        _, step, a, b = spans[which]
        to, frm = steps[step]
        count = (b - a) * PIECE
        shift = (a - step * per) * PIECE
        at_row = (frm if arriving else me) * (per * PIECE) + shift
        lanes = pl.ds(pl.multiple_of(half * (3 * part), 3 * part), 3 * part)
        return pltpu.make_async_remote_copy(
            src_ref=send.at[pl.ds(a * PIECE, count), lanes],
            dst_ref=recv.at[pl.ds(pl.multiple_of(at_row, PIECE), count), lanes],
            send_sem=send_sem.at[which, half],
            recv_sem=recv_sem.at[which, half],
            device_id={"enc": to},
            device_id_type=MESH,
        )

    pl.semaphore_wait(barrier, n - 1 + groups - 1)
    for chunk in range(pmax // UNIT):
        unit(
            chunk,
            lambda half: [
                span_copy(w, half, False) for w in range(len(spans)) if spans[w][0] == chunk
            ],
        )
    own = pltpu.make_async_copy(
        send.at[pl.ds((n - 1) * per * PIECE, per * PIECE)],
        recv.at[pl.ds(pl.multiple_of(me * (per * PIECE), PIECE), per * PIECE)],
        own_sem,
    )
    own.start()

    gq = jnp.sum(acc[0:8, :], 0, keepdims=True)
    gk = jnp.sum(acc[8:16, :], 0, keepdims=True)
    for j in range(groups):
        gpart[j, 0:1, 0:width] = gq[:, j * width : (j + 1) * width]
        gpart[j, 1:2, 0:width] = gk[:, j * width : (j + 1) * width]
    shares = []
    for off in range(1, groups):
        to = lax.rem(grp + off, groups)
        share = pltpu.make_async_remote_copy(
            src_ref=gpart.at[to],
            dst_ref=grecv.at[off],
            send_sem=gs_sem.at[off],
            recv_sem=gr_sem.at[off],
            device_id={"grp": to},
            device_id_type=MESH,
        )
        share.start()
        shares.append(share)
    mine = gpart[grp]
    for off, share in enumerate(shares, 1):
        share.wait_recv()
        mine = mine + grecv[off]
    erecv[me] = mine
    sums = []
    for i, (to, frm) in enumerate(steps[:-1]):
        both_ways = [
            pltpu.make_async_remote_copy(
                src_ref=erecv.at[me],
                dst_ref=erecv.at[at],
                send_sem=es_sem.at[i],
                recv_sem=er_sem.at[i],
                device_id={"enc": to},
                device_id_type=MESH,
            )
            for at in (me, frm)
        ]
        both_ways[0].start()
        sums.append(both_ways)
    index = [0] * P_OWN
    start = 0
    for s in range(n):
        got = 0
        for j in range(pmax):
            got = got + (plan_ref[0, s, j] == me).astype(jnp.int32)
        for p in range(P_OWN):
            inside = jnp.logical_and(p >= start, p < start + got)
            index[p] = jnp.where(inside, s * per + p - start, index[p])
        start = start + got
    for out, arrived in sums:
        arrived.wait_recv()
    total = erecv[0]
    for s in range(1, n):
        total = total + erecv[s]
    og_ref[...] = total[0:2, 0:width] / math.sqrt(n * groups * P_OWN * PIECE)

    orow = lax.broadcasted_iota(jnp.int32, (P_OWN * PIECE, pmax * PIECE), 0)
    olane = lax.broadcasted_iota(jnp.int32, (P_OWN * PIECE, pmax * PIECE), 1)
    base = index[-1] * PIECE
    for p in range(P_OWN - 2, -1, -1):
        base = jnp.where(orow < (p + 1) * PIECE, index[p] * PIECE, base)
    order_ref[...] = (olane == base + lax.rem(orow, PIECE)).astype(F32).astype(BF)
    small = [
        pltpu.make_async_copy(order_ref, order_hbm, out_sem.at[0]),
        pltpu.make_async_copy(og_ref, og_hbm, out_sem.at[1]),
    ]
    for copy in small:
        copy.start()
    own.wait()
    for copy in small:
        copy.wait()
    for half in range(halves_count):
        for w in range(len(spans)):
            span_copy(w, half, True).wait_recv()
    for half in range(halves_count):
        for w in range(len(spans)):
            span_copy(w, half, False).wait_send()
    for share in shares:
        share.wait_send()
    for out, _ in sums:
        out.wait_send()


def place(recv_hbm, order_hbm, gain, oq, ok, ov, og, recv, order, buf, in_sem, sem):
    feat = oq.shape[1]
    part = PAIRS * LANES
    count = feat // part
    first = pltpu.make_async_copy(order_hbm, order, in_sem.at[3 * count])
    first.start()
    loads = []
    for a in range(3):
        for half in range(count):
            low = half * (3 * part) + a * part
            lanes = slice(low, low + part)
            loads.append(
                pltpu.make_async_copy(
                    recv_hbm.at[:, lanes], recv.at[:, lanes], in_sem.at[a * count + half]
                )
            )
            loads[-1].start()
    copies = [pltpu.make_async_copy(gain, og, sem.at[3])]
    copies[0].start()
    first.wait()
    pick = order[...]
    for a, out in enumerate((oq, ok, ov)):
        for half in range(count):
            loads[a * count + half].wait()
            low = half * (3 * part) + a * part
            buf[a, :, half * part : (half + 1) * part] = dot(
                pick, recv[:, low : low + part]
            ).astype(BF)
        copies.append(pltpu.make_async_copy(buf.at[a], out, sem.at[a]))
        copies[-1].start()
    for copy in copies:
        copy.wait()


PAIRS = 2


def local(query_raw, key_raw, value_rows, out_cotangent, image_ids, owners, gains):
    n = lax.axis_size("enc")
    groups = lax.axis_size("grp")
    pmax = owners.shape[-1]
    rows, feat = query_raw.shape
    own_rows = P_OWN * PIECE
    hbm = pl.BlockSpec(memory_space=pltpu.HBM)
    grad = jax.ShapeDtypeStruct((own_rows, feat), BF)
    gain = jax.ShapeDtypeStruct((2, feat // groups), F32)
    dma = pltpu.SemaphoreType.DMA
    many = n + pmax // UNIT
    halves_count = feat // (PAIRS * LANES)
    arrived, order, share = pl.pallas_call(
        functools.partial(kernel, n, groups, pmax),
        out_shape=(
            jax.ShapeDtypeStruct((rows, 3 * feat), BF),
            jax.ShapeDtypeStruct((own_rows, rows), BF),
            gain,
        ),
        in_specs=[hbm] * 7,
        out_specs=(hbm,) * 3,
        scratch_shapes=[pltpu.VMEM((rows, feat), BF)] * 4
        + [
            pltpu.VMEM((1, rows), jnp.int32),
            pltpu.SMEM(owners.shape, jnp.int32),
            pltpu.VMEM(gains.shape, F32),
            pltpu.VMEM((own_rows, rows), BF),
            pltpu.VMEM(gain.shape, F32),
            pltpu.VMEM((rows, 3 * feat), BF),
            pltpu.VMEM((16, feat), F32),
            pltpu.VMEM((groups, 8, LANES), F32),
            pltpu.VMEM((groups, 8, LANES), F32),
            pltpu.VMEM((n, 8, LANES), F32),
            dma((7,)),
            dma((2,)),
            dma,
            dma((many, halves_count)),
            dma((many, halves_count)),
            dma((groups,)),
            dma((groups,)),
            dma((n,)),
            dma((n,)),
        ],
        compiler_params=pltpu.CompilerParams(
            collective_id=0, has_side_effects=True, vmem_limit_bytes=62 * 1024 * 1024
        ),
        cost_estimate=pl.CostEstimate(
            flops=2 * 24 * rows * feat * LANES,
            bytes_accessed=14 * rows * feat,
            transcendentals=rows * feat,
        ),
    )(query_raw, key_raw, value_rows, out_cotangent, image_ids.reshape(1, rows), owners, gains)
    return pl.pallas_call(
        place,
        out_shape=(grad, grad, grad, gain),
        in_specs=[hbm] * 3,
        out_specs=(hbm,) * 4,
        scratch_shapes=[
            pltpu.VMEM((rows, 3 * feat), BF),
            pltpu.VMEM((own_rows, rows), BF),
            pltpu.VMEM((3, own_rows, feat), BF),
            dma((3 * halves_count + 1,)),
            dma((4,)),
        ],
        compiler_params=pltpu.CompilerParams(vmem_limit_bytes=62 * 1024 * 1024),
    )(arrived, order, share)


def solution(mesh):
    rows = P(("enc", "grp"), None)
    return jax.shard_map(
        local,
        mesh=mesh,
        in_specs=(rows, rows, rows, rows, P(("enc", "grp")), P("grp", None, None), P()),
        out_specs=(rows, rows, rows, P(None, "grp")),
        check_vma=False,
    )
```
